32 devices in a mesh: row: 2 (over y), col: 4 (over x, core), rep: 4 (over z).
Axes of the slice: x: 2, y: 2, z: 4, core: 2. Of those that a mesh axis runs over, the one named last changes fastest.
Arguments:
- amplitudes: bfloat16 [384, 100, 1024], P(('row', 'col'), 'rep'), may hold values from -6 to 6
- integrals: bfloat16 [100, 1024, 256], P('rep', 'col', 'row'), may hold values from -0.02734375 to 0.02734375
Outputs:
- cycle: float32 [384, 256], P('row', ('col', 'rep'))
The draws below stay inside these ranges and needn't reach their ends.
All inputs are finite; a program needn't handle non-finite values.
Results may differ from the reference program's by a relative error of at most 0.0003.
Values may be sent and summed in bfloat16 or wider, within the bound.
A program may use at most 64 MiB of HBM per device.

```python
import jax
import jax.numpy as jnp
from jax import lax

O = 100
V = 1024
ROWS = 384
COLS = 256


def strengthened(array, key, source, target, blocks, factor):
    def block_of(position):
        return (jnp.arange(array.shape[position]) // (array.shape[position] // blocks)).reshape((-1,) + (1,) * (array.ndim - 1 - position))

    near = jax.random.permutation(key, blocks)[block_of(target)]
    other_side = (block_of(target) + blocks // 2) % blocks
    return jnp.where((block_of(source) == near) | (block_of(source) == other_side), factor * array, array)


def shard_levels(key, extent, shards, smallest, largest):
    level = 1.0
    for dim, parts in shards:
        steps = jax.random.uniform(jax.random.fold_in(jax.random.fold_in(key, 6), dim), (parts,), jnp.float32, smallest / len(shards), largest / len(shards))
        level = level * jnp.repeat(jnp.exp(steps), extent[dim] // parts).reshape((-1,) + (1,) * (len(extent) - 1 - dim))
    return level


def noise(own_key, dims, deviation, bound, split=(), kind=jnp.bfloat16):
    entries = deviation * jax.random.normal(own_key, dims, jnp.float32)
    if split:
        entries = entries * shard_levels(own_key, dims, split, -0.22, 0.18)
    return jnp.clip(entries, -bound, bound).astype(kind)


def gaussian_with(own_key, shape, spread, reach, cuts, heavy, held_as=jnp.bfloat16):
    entries = spread * jax.random.normal(own_key, shape, jnp.float32)
    if cuts:
        entries = entries * shard_levels(own_key, shape, cuts, -0.22, 0.18)
    return jnp.clip(strengthened(entries, jax.random.fold_in(own_key, 3), *heavy), -reach, reach).astype(held_as)


def setup_inputs(seed: int = 0) -> dict:
    arg_keys = jax.random.split(jax.random.key(seed), 3)
    amplitudes = noise(arg_keys[0], (ROWS, O, V), 1.0, 6.0, ((0, 8), (1, 4)))
    integrals = gaussian_with(arg_keys[1], (O, V, COLS), (O * V) ** -0.5, 0.02734375, ((0, 4), (1, 4), (2, 2)), (1, 2, 4, 2.0))
    return dict(amplitudes=amplitudes, integrals=integrals)


def reference(amplitudes, integrals):
    def accumulate(running, orbital):
        amp_slab = lax.dynamic_index_in_dim(amplitudes, orbital, 1, keepdims=False)
        int_slab = lax.dynamic_index_in_dim(integrals, orbital, 0, keepdims=False)
        running = running + jnp.dot(amp_slab, int_slab, preferred_element_type=jnp.float32)
        return running, None

    initial = jnp.zeros((ROWS, COLS), jnp.float32)
    result, unused = lax.scan(accumulate, initial, jnp.arange(O, dtype=jnp.int32))
    return result
```

```python
import functools

import jax
import jax.numpy as jnp
from jax import lax
from jax.experimental import pallas as pl
from jax.experimental.pallas import tpu as pltpu
from jax.sharding import PartitionSpec as P

MESH = pl.DeviceIdType.MESH


def chunk_bounds(depth):
    count = min(5, depth)
    edges = [depth * i // count for i in range(count + 1)]
    return list(zip(edges[:-1], edges[1:]))


def kernel(sizes, split, a_ref, b_ref, o_ref, a_buf, b_buf, parts, inbox,
           a_send, a_recv, b_send, b_recv, p_send, p_recv, own_sem):
    rows, cols, reps = sizes
    row, col, rep = lax.axis_index("row"), lax.axis_index("col"), lax.axis_index("rep")
    group = cols * reps
    me = col * reps + rep
    depth, height, width = a_buf.shape[1:]
    lanes = b_buf.shape[3]
    share = parts.shape[1]
    per = lanes // share
    total_rows = cols * height
    bounds = chunk_bounds(depth)

    def row_at(d):
        return lax.rem(row + d, rows)

    def col_at(d):
        return lax.rem(col + d, cols)

    barrier = pltpu.get_barrier_semaphore()
    for d in range(1, rows):
        pl.semaphore_signal(barrier, inc=1, device_id={"row": row_at(d)}, device_id_type=MESH)
    for d in range(1, group):
        other = lax.rem(me + d, group)
        pl.semaphore_signal(barrier, inc=1, device_id={"col": other // reps, "rep": lax.rem(other, reps)},
                            device_id_type=MESH)

    def piece(lo, hi, owner):
        if split:
            return a_ref.at[owner, lo:hi]
        return a_ref.at[lo:hi, :, pl.ds(pl.multiple_of(owner * width, width), width)]

    own_a = pltpu.make_async_copy(piece(0, depth, col), a_buf.at[col], own_sem.at[0])
    own_b = pltpu.make_async_copy(b_ref, b_buf.at[row], own_sem.at[1])
    own_a.start()
    own_b.start()
    pl.semaphore_wait(barrier, rows - 1 + group - 1)

    a_copies, b_copies = [], []
    for g, (lo, hi) in enumerate(bounds):
        b_copies.append([])
        for d in range(1, rows):
            copy = pltpu.make_async_remote_copy(
                src_ref=b_ref.at[lo:hi], dst_ref=b_buf.at[row, lo:hi],
                send_sem=b_send.at[d - 1, g], recv_sem=b_recv.at[d - 1, g],
                device_id={"row": row_at(d)}, device_id_type=MESH)
            copy.start()
            b_copies[-1].append(copy)
        a_copies.append([])
        for d in range(1, cols):
            copy = pltpu.make_async_remote_copy(
                src_ref=piece(lo, hi, col_at(d)), dst_ref=a_buf.at[col, lo:hi],
                send_sem=a_send.at[d - 1, g], recv_sem=a_recv.at[d - 1, g],
                device_id={"col": col_at(d)}, device_id_type=MESH)
            copy.start()
            a_copies[-1].append(copy)

    def product(lo, hi, source):
        left = jnp.concatenate(
            [jnp.concatenate([a_buf[c, k] for c in range(cols)], axis=0) for k in range(lo, hi)], axis=1)
        right = jnp.concatenate([b_buf[source, k] for k in range(lo, hi)], axis=0)
        return jnp.dot(left, right, preferred_element_type=jnp.float32)

    def part_copy(owner):
        return pltpu.make_async_remote_copy(
            src_ref=parts.at[owner], dst_ref=inbox.at[me],
            send_sem=p_send.at[owner], recv_sem=p_recv.at[me],
            device_id={"col": owner // reps, "rep": lax.rem(owner, reps)}, device_id_type=MESH)

    def hand_out(source, value):
        parts[pl.ds(source * per, per)] = value.T.reshape(per, share, total_rows)
        for i in range(per):
            owner = source * per + i

            @pl.when(owner != me)
            def _():
                part_copy(owner).start()

    own_a.wait()
    own_b.wait()
    value = None
    for g, (lo, hi) in enumerate(bounds):
        for copy in a_copies[g]:
            copy.wait_recv()
        term = product(lo, hi, row)
        value = term if value is None else value + term
    hand_out(row, value)

    for d in range(1, rows):
        source = lax.rem(row + rows - d, rows)
        value = None
        for g, (lo, hi) in enumerate(bounds):
            b_copies[g][d - 1].wait_recv()
            term = product(lo, hi, source)
            value = term if value is None else value + term
        hand_out(source, value)

    result = parts[me]
    for d in range(1, group):
        source = lax.rem(me + d, group)
        pltpu.make_async_remote_copy(
            src_ref=parts.at[source], dst_ref=inbox.at[source],
            send_sem=p_send.at[source], recv_sem=p_recv.at[source],
            device_id={"col": source // reps, "rep": lax.rem(source, reps)}, device_id_type=MESH).wait_recv()
        result = result + inbox[source]
    o_ref[...] = result

    for copies in a_copies + b_copies:
        for copy in copies:
            copy.wait_send()
    for d in range(1, group):
        part_copy(lax.rem(me + d, group)).wait_send()


def local(sizes, amplitudes, integrals):
    rows, cols, reps = sizes
    height, depth, virtuals = amplitudes.shape
    width, lanes = integrals.shape[1:]
    group = cols * reps
    share = rows * lanes // group
    chunks = len(chunk_bounds(depth))
    split = width % 128 != 0
    blocks = jnp.transpose(amplitudes, (1, 0, 2))
    if split:
        blocks = jnp.transpose(blocks.reshape(depth, height, cols, width), (2, 0, 1, 3))
    dma = pltpu.SemaphoreType.DMA
    summed = pl.pallas_call(
        functools.partial(kernel, sizes, split),
        out_shape=jax.ShapeDtypeStruct((share, cols * height), jnp.float32),
        in_specs=[pl.BlockSpec(memory_space=pl.ANY)] * 2,
        out_specs=pl.BlockSpec(memory_space=pltpu.VMEM),
        scratch_shapes=[
            pltpu.VMEM((cols, depth, height, width), amplitudes.dtype),
            pltpu.VMEM((rows, depth, width, lanes), integrals.dtype),
            pltpu.VMEM((group, share, cols * height), jnp.float32),
            pltpu.VMEM((group, share, cols * height), jnp.float32),
            dma((max(cols - 1, 1), chunks)),
            dma((max(cols - 1, 1), chunks)),
            dma((max(rows - 1, 1), chunks)),
            dma((max(rows - 1, 1), chunks)),
            dma((group,)),
            dma((group,)),
            dma((2,)),
        ],
        compiler_params=pltpu.CompilerParams(
            collective_id=0, has_side_effects=True, vmem_limit_bytes=56 * 1024 * 1024),
        cost_estimate=pl.CostEstimate(
            flops=2 * cols * height * rows * lanes * depth * width,
            bytes_accessed=2 * (amplitudes.size + integrals.size), transcendentals=0),
    )(blocks, integrals)
    return summed.T


def solution(mesh):
    sizes = (mesh.shape["row"], mesh.shape["col"], mesh.shape["rep"])
    return jax.shard_map(
        functools.partial(local, sizes),
        mesh=mesh,
        in_specs=(P(("row", "col"), "rep", None), P("rep", "col", "row")),
        out_specs=P("row", ("col", "rep")),
        check_vma=False,
    )
```

```python
import functools

import jax
import jax.numpy as jnp
from jax import lax
from jax.experimental import pallas as pl
from jax.experimental.pallas import tpu as pltpu
from jax.sharding import PartitionSpec as P

MESH = pl.DeviceIdType.MESH


def chunk_bounds(depth):
    edges = sorted({0, depth * 6 // 25, depth * 12 // 25, depth * 18 // 25, depth * 22 // 25, depth - 1, depth})
    return list(zip(edges[:-1], edges[1:]))


def kernel(sizes, split, a_ref, b_ref, o_ref, a_buf, b_buf, parts, inbox,
           a_send, a_recv, b_send, b_recv, p_send, p_recv, own_sem):
    rows, cols, reps = sizes
    row, col, rep = lax.axis_index("row"), lax.axis_index("col"), lax.axis_index("rep")
    group = cols * reps
    me = col * reps + rep
    depth, height, width = a_buf.shape[1:]
    lanes = b_buf.shape[3]
    share = parts.shape[1]
    per = lanes // share
    total_rows = cols * height
    bounds = chunk_bounds(depth)

    def row_at(d):
        return lax.rem(row + d, rows)

    def col_at(d):
        return lax.rem(col + d, cols)

    barrier = pltpu.get_barrier_semaphore()
    for d in range(1, rows):
        pl.semaphore_signal(barrier, inc=1, device_id={"row": row_at(d)}, device_id_type=MESH)
    for d in range(1, group):
        other = lax.rem(me + d, group)
        pl.semaphore_signal(barrier, inc=1, device_id={"col": other // reps, "rep": lax.rem(other, reps)},
                            device_id_type=MESH)

    def piece(lo, hi, owner):
        if split:
            return a_ref.at[owner, lo:hi]
        return a_ref.at[lo:hi, :, pl.ds(pl.multiple_of(owner * width, width), width)]

    own_a = pltpu.make_async_copy(piece(0, depth, col), a_buf.at[col], own_sem.at[0])
    own_b = pltpu.make_async_copy(b_ref, b_buf.at[row], own_sem.at[1])
    own_a.start()
    own_b.start()
    pl.semaphore_wait(barrier, rows - 1 + group - 1)

    a_copies, b_copies = [], []
    for g, (lo, hi) in enumerate(bounds):
        b_copies.append([])
        for d in range(1, rows):
            copy = pltpu.make_async_remote_copy(
                src_ref=b_ref.at[lo:hi], dst_ref=b_buf.at[row, lo:hi],
                send_sem=b_send.at[d - 1, g], recv_sem=b_recv.at[d - 1, g],
                device_id={"row": row_at(d)}, device_id_type=MESH)
            copy.start()
            b_copies[-1].append(copy)
        a_copies.append([])
        for d in range(1, cols):
            copy = pltpu.make_async_remote_copy(
                src_ref=piece(lo, hi, col_at(d)), dst_ref=a_buf.at[col, lo:hi],
                send_sem=a_send.at[d - 1, g], recv_sem=a_recv.at[d - 1, g],
                device_id={"col": col_at(d)}, device_id_type=MESH)
            copy.start()
            a_copies[-1].append(copy)

    def product(lo, hi, source):
        left = jnp.concatenate(
            [jnp.concatenate([a_buf[c, k] for c in range(cols)], axis=0) for k in range(lo, hi)], axis=1)
        right = jnp.concatenate([b_buf[source, k] for k in range(lo, hi)], axis=0)
        return jnp.dot(left, right, preferred_element_type=jnp.float32)

    def part_copy(owner):
        return pltpu.make_async_remote_copy(
            src_ref=parts.at[owner], dst_ref=inbox.at[lax.rem(owner - me + group, group) - 1],
            send_sem=p_send, recv_sem=p_recv,
            device_id={"col": owner // reps, "rep": lax.rem(owner, reps)}, device_id_type=MESH)

    def hand_out(source, value):
        parts[pl.ds(source * per, per)] = value.T.reshape(per, share, total_rows)
        for i in range(per):
            owner = source * per + i

            @pl.when(owner != me)
            def _():
                part_copy(owner).start()

    own_a.wait()
    own_b.wait()
    value = None
    for g, (lo, hi) in enumerate(bounds):
        for copy in a_copies[g]:
            copy.wait_recv()
        term = product(lo, hi, row)
        value = term if value is None else value + term
    hand_out(row, value)

    for copies in a_copies:
        for copy in copies:
            copy.wait_send()

    for d in range(1, rows):
        source = lax.rem(row + rows - d, rows)
        value = None
        for g, (lo, hi) in enumerate(bounds):
            if g > 0:
                b_copies[g - 1][d - 1].wait_send()
            b_copies[g][d - 1].wait_recv()
            term = product(lo, hi, source)
            value = term if value is None else value + term
        hand_out(source, value)

    pieces = pltpu.make_async_remote_copy(
        src_ref=parts.at[0:group - 1], dst_ref=inbox, send_sem=p_send, recv_sem=p_recv,
        device_id={"col": col_at(1)}, device_id_type=MESH)
    pieces.wait_recv()
    result = parts[me]
    for i in range(group - 1):
        result = result + inbox[i]
    o_ref[...] = result

    for copy in b_copies[-1]:
        copy.wait_send()
    pieces.wait_send()


def local(sizes, amplitudes, integrals):
    rows, cols, reps = sizes
    height, depth, virtuals = amplitudes.shape
    width, lanes = integrals.shape[1:]
    group = cols * reps
    share = rows * lanes // group
    chunks = len(chunk_bounds(depth))
    split = width % 128 != 0
    blocks = jnp.transpose(amplitudes, (1, 0, 2))
    if split:
        blocks = jnp.transpose(blocks.reshape(depth, height, cols, width), (2, 0, 1, 3))
    dma = pltpu.SemaphoreType.DMA
    summed = pl.pallas_call(
        functools.partial(kernel, sizes, split),
        out_shape=jax.ShapeDtypeStruct((share, cols * height), jnp.float32),
        in_specs=[pl.BlockSpec(memory_space=pl.ANY)] * 2,
        out_specs=pl.BlockSpec(memory_space=pltpu.VMEM),
        scratch_shapes=[
            pltpu.VMEM((cols, depth, height, width), amplitudes.dtype),
            pltpu.VMEM((rows, depth, width, lanes), integrals.dtype),
            pltpu.VMEM((group, share, cols * height), jnp.float32),
            pltpu.VMEM((group - 1, share, cols * height), jnp.float32),
            dma((max(cols - 1, 1), chunks)),
            dma((max(cols - 1, 1), chunks)),
            dma((max(rows - 1, 1), chunks)),
            dma((max(rows - 1, 1), chunks)),
            dma,
            dma,
            dma((2,)),
        ],
        compiler_params=pltpu.CompilerParams(
            collective_id=0, has_side_effects=True, vmem_limit_bytes=56 * 1024 * 1024),
        cost_estimate=pl.CostEstimate(
            flops=2 * cols * height * rows * lanes * depth * width,
            bytes_accessed=2 * (amplitudes.size + integrals.size), transcendentals=0),
    )(blocks, integrals)
    return summed.T


def solution(mesh):
    sizes = (mesh.shape["row"], mesh.shape["col"], mesh.shape["rep"])
    return jax.shard_map(
        functools.partial(local, sizes),
        mesh=mesh,
        in_specs=(P(("row", "col"), "rep", None), P("rep", "col", "row")),
        out_specs=P("row", ("col", "rep")),
        check_vma=False,
    )
```

```python
import functools

import jax
import jax.numpy as jnp
from jax import lax
from jax.experimental import pallas as pl
from jax.experimental.pallas import tpu as pltpu
from jax.sharding import PartitionSpec as P

MESH = pl.DeviceIdType.MESH


def chunk_bounds(depth):
    edges = sorted({0, depth * 6 // 25, depth * 12 // 25, depth * 18 // 25, depth * 22 // 25, depth - 1, depth})
    return list(zip(edges[:-1], edges[1:]))


def kernel(sizes, split, a_ref, b_ref, o_ref, a_buf, b_buf, parts, inbox,
           a_send, a_recv, b_send, b_recv, p_send, p_recv, own_sem):
    rows, cols, reps = sizes
    row, col, rep = lax.axis_index("row"), lax.axis_index("col"), lax.axis_index("rep")
    group = cols * reps
    me = col * reps + rep
    depth, height, width = a_buf.shape[1:]
    lanes = b_buf.shape[3]
    share = parts.shape[1]
    per = lanes // share
    total_rows = cols * height
    bounds = chunk_bounds(depth)

    def row_at(d):
        return lax.rem(row + d, rows)

    def col_at(d):
        return lax.rem(col + d, cols)

    barrier = pltpu.get_barrier_semaphore()
    for d in range(1, rows):
        pl.semaphore_signal(barrier, inc=1, device_id={"row": row_at(d)}, device_id_type=MESH)
    for d in range(1, group):
        other = lax.rem(me + d, group)
        pl.semaphore_signal(barrier, inc=1, device_id={"col": other // reps, "rep": lax.rem(other, reps)},
                            device_id_type=MESH)

    def piece(lo, hi, owner):
        if split:
            return a_ref.at[owner, lo:hi]
        return a_ref.at[lo:hi, :, pl.ds(pl.multiple_of(owner * width, width), width)]

    own_a = pltpu.make_async_copy(piece(0, depth, col), a_buf.at[col], own_sem.at[0])
    own_b = pltpu.make_async_copy(b_ref, b_buf.at[row], own_sem.at[1])
    pl.semaphore_wait(barrier, rows - 1 + group - 1)

    a_copies, b_copies = [], []
    for g, (lo, hi) in enumerate(bounds):
        b_copies.append([])
        for d in range(1, rows):
            copy = pltpu.make_async_remote_copy(
                src_ref=b_ref.at[lo:hi], dst_ref=b_buf.at[row, lo:hi],
                send_sem=b_send.at[d - 1, g], recv_sem=b_recv.at[d - 1, g],
                device_id={"row": row_at(d)}, device_id_type=MESH)
            copy.start()
            b_copies[-1].append(copy)
    for g, (lo, hi) in enumerate(bounds):
        a_copies.append([])
        for d in range(1, cols):
            copy = pltpu.make_async_remote_copy(
                src_ref=piece(lo, hi, col_at(d)), dst_ref=a_buf.at[col, lo:hi],
                send_sem=a_send.at[d - 1, g], recv_sem=a_recv.at[d - 1, g],
                device_id={"col": col_at(d)}, device_id_type=MESH)
            copy.start()
            a_copies[-1].append(copy)

    own_a.start()
    own_b.start()

    def product(lo, hi, source):
        left = jnp.concatenate(
            [jnp.concatenate([a_buf[c, k] for c in range(cols)], axis=0) for k in range(lo, hi)], axis=1)
        right = jnp.concatenate([b_buf[source, k] for k in range(lo, hi)], axis=0)
        return jnp.dot(left, right, preferred_element_type=jnp.float32)

    def part_copy(owner):
        return pltpu.make_async_remote_copy(
            src_ref=parts.at[owner], dst_ref=inbox.at[lax.rem(owner - me + group, group) - 1],
            send_sem=p_send, recv_sem=p_recv,
            device_id={"col": owner // reps, "rep": lax.rem(owner, reps)}, device_id_type=MESH)

    def hand_out(source, value):
        parts[pl.ds(source * per, per)] = value.T.reshape(per, share, total_rows)
        for i in range(per):
            owner = source * per + i

            @pl.when(owner != me)
            def _():
                part_copy(owner).start()

    own_a.wait()
    own_b.wait()
    value = None
    for g, (lo, hi) in enumerate(bounds):
        for copy in a_copies[g]:
            copy.wait_recv()
        term = product(lo, hi, row)
        value = term if value is None else value + term
    hand_out(row, value)

    for copies in a_copies:
        for copy in copies:
            copy.wait_send()

    for d in range(1, rows):
        source = lax.rem(row + rows - d, rows)
        value = None
        for g, (lo, hi) in enumerate(bounds):
            if g > 0:
                b_copies[g - 1][d - 1].wait_send()
            b_copies[g][d - 1].wait_recv()
            term = product(lo, hi, source)
            value = term if value is None else value + term
        hand_out(source, value)

    pieces = pltpu.make_async_remote_copy(
        src_ref=parts.at[0:group - 1], dst_ref=inbox, send_sem=p_send, recv_sem=p_recv,
        device_id={"col": col_at(1)}, device_id_type=MESH)
    pieces.wait_recv()
    result = parts[me]
    for i in range(group - 1):
        result = result + inbox[i]
    o_ref[...] = result

    for copy in b_copies[-1]:
        copy.wait_send()
    pieces.wait_send()


def local(sizes, amplitudes, integrals):
    rows, cols, reps = sizes
    height, depth, virtuals = amplitudes.shape
    width, lanes = integrals.shape[1:]
    group = cols * reps
    share = rows * lanes // group
    chunks = len(chunk_bounds(depth))
    split = width % 128 != 0
    blocks = jnp.transpose(amplitudes, (1, 0, 2))
    if split:
        blocks = jnp.transpose(blocks.reshape(depth, height, cols, width), (2, 0, 1, 3))
    dma = pltpu.SemaphoreType.DMA
    summed = pl.pallas_call(
        functools.partial(kernel, sizes, split),
        out_shape=jax.ShapeDtypeStruct((share, cols * height), jnp.float32),
        in_specs=[pl.BlockSpec(memory_space=pl.ANY)] * 2,
        out_specs=pl.BlockSpec(memory_space=pltpu.VMEM),
        scratch_shapes=[
            pltpu.VMEM((cols, depth, height, width), amplitudes.dtype),
            pltpu.VMEM((rows, depth, width, lanes), integrals.dtype),
            pltpu.VMEM((group, share, cols * height), jnp.float32),
            pltpu.VMEM((group - 1, share, cols * height), jnp.float32),
            dma((max(cols - 1, 1), chunks)),
            dma((max(cols - 1, 1), chunks)),
            dma((max(rows - 1, 1), chunks)),
            dma((max(rows - 1, 1), chunks)),
            dma,
            dma,
            dma((2,)),
        ],
        compiler_params=pltpu.CompilerParams(
            collective_id=0, has_side_effects=True, vmem_limit_bytes=56 * 1024 * 1024),
        cost_estimate=pl.CostEstimate(
            flops=2 * cols * height * rows * lanes * depth * width,
            bytes_accessed=2 * (amplitudes.size + integrals.size), transcendentals=0),
    )(blocks, integrals)
    return summed.T


def solution(mesh):
    sizes = (mesh.shape["row"], mesh.shape["col"], mesh.shape["rep"])
    return jax.shard_map(
        functools.partial(local, sizes),
        mesh=mesh,
        in_specs=(P(("row", "col"), "rep", None), P("rep", "col", "row")),
        out_specs=P("row", ("col", "rep")),
        check_vma=False,
    )
```

```python
import functools

import jax
import jax.numpy as jnp
from jax import lax
from jax.experimental import pallas as pl
from jax.experimental.pallas import tpu as pltpu
from jax.sharding import PartitionSpec as P

MESH = pl.DeviceIdType.MESH


def chunk_bounds(depth):
    edges = sorted({0, depth * 6 // 25, depth * 12 // 25, depth * 18 // 25, depth * 22 // 25, depth - 1, depth})
    return list(zip(edges[:-1], edges[1:]))


def kernel(sizes, split, a_ref, b_ref, o_ref, a_buf, b_buf, parts, z_inbox, mid, c_inbox, mine,
           a_send, a_recv, b_send, b_recv, z_send, z_recv, c_send, c_recv, own_sem):
    rows, cols, reps = sizes
    row, col, rep = lax.axis_index("row"), lax.axis_index("col"), lax.axis_index("rep")
    depth, height, width = a_buf.shape[1:]
    near, share, total_rows = parts.shape[2:]
    bounds = chunk_bounds(depth)

    def row_at(d):
        return lax.rem(row + d, rows)

    def col_at(d):
        return lax.rem(col + d, cols)

    def rep_at(d):
        return lax.rem(rep + d, reps)

    barrier = pltpu.get_barrier_semaphore()
    for d in range(1, rows):
        pl.semaphore_signal(barrier, inc=1, device_id={"row": row_at(d)}, device_id_type=MESH)
    for d in range(1, cols):
        pl.semaphore_signal(barrier, inc=1, device_id={"col": col_at(d)}, device_id_type=MESH)
    for d in range(1, reps):
        pl.semaphore_signal(barrier, inc=1, device_id={"rep": rep_at(d)}, device_id_type=MESH)

    def piece(lo, hi, owner):
        if split:
            return a_ref.at[owner, lo:hi]
        return a_ref.at[lo:hi, :, pl.ds(pl.multiple_of(owner * width, width), width)]

    own_a = pltpu.make_async_copy(piece(0, depth, col), a_buf.at[col], own_sem.at[0])
    own_b = pltpu.make_async_copy(b_ref, b_buf.at[row], own_sem.at[1])
    pl.semaphore_wait(barrier, rows + cols + reps - 3)

    a_copies, b_copies = [], []
    for g, (lo, hi) in enumerate(bounds):
        b_copies.append([])
        for d in range(1, rows):
            copy = pltpu.make_async_remote_copy(
                src_ref=b_ref.at[lo:hi], dst_ref=b_buf.at[row, lo:hi],
                send_sem=b_send.at[d - 1, g], recv_sem=b_recv.at[d - 1, g],
                device_id={"row": row_at(d)}, device_id_type=MESH)
            copy.start()
            b_copies[-1].append(copy)
    for g, (lo, hi) in enumerate(bounds):
        a_copies.append([])
        for d in range(1, cols):
            copy = pltpu.make_async_remote_copy(
                src_ref=piece(lo, hi, col_at(d)), dst_ref=a_buf.at[col, lo:hi],
                send_sem=a_send.at[d - 1, g], recv_sem=a_recv.at[d - 1, g],
                device_id={"col": col_at(d)}, device_id_type=MESH)
            copy.start()
            a_copies[-1].append(copy)

    own_a.start()
    own_b.start()

    def product(lo, hi, source):
        left = jnp.concatenate(
            [jnp.concatenate([a_buf[c, k] for c in range(cols)], axis=0) for k in range(lo, hi)], axis=1)
        right = jnp.concatenate([b_buf[source, k] for k in range(lo, hi)], axis=0)
        return jnp.dot(left, right, preferred_element_type=jnp.float32)

    def over_reps(h, value):
        pieces = value.T.reshape(near, reps, share, total_rows)
        for z in range(reps):
            parts[h, z] = pieces[:, z]
        for d in range(1, reps):
            pltpu.make_async_remote_copy(
                src_ref=parts.at[h, rep_at(d)], dst_ref=z_inbox.at[h, d - 1],
                send_sem=z_send.at[h], recv_sem=z_recv.at[h],
                device_id={"rep": rep_at(d)}, device_id_type=MESH).start()

    def over_cols(h):
        arrived = pltpu.make_async_remote_copy(
            src_ref=parts.at[h, 0:reps - 1], dst_ref=z_inbox.at[h], send_sem=z_send.at[h], recv_sem=z_recv.at[h],
            device_id={"rep": rep_at(1)}, device_id_type=MESH)
        arrived.wait_recv()
        total = parts[h, rep]
        for d in range(reps - 1):
            total = total + z_inbox[h, d]
        mid[h] = total
        for i in range(near):
            owner = lax.rem(row + rows - h, rows) * near + i

            @pl.when(owner != col)
            def _():
                pltpu.make_async_remote_copy(
                    src_ref=mid.at[h, i], dst_ref=c_inbox.at[lax.rem(owner - col + cols, cols) - 1],
                    send_sem=c_send, recv_sem=c_recv, device_id={"col": owner}, device_id_type=MESH).start()

            @pl.when(owner == col)
            def _():
                mine[...] = mid[h, i]
        return arrived

    own_a.wait()
    own_b.wait()
    value = None
    for g, (lo, hi) in enumerate(bounds):
        for copy in a_copies[g]:
            copy.wait_recv()
        term = product(lo, hi, row)
        value = term if value is None else value + term
    over_reps(0, value)

    for copies in a_copies:
        for copy in copies:
            copy.wait_send()

    reduced = []
    for d in range(1, rows):
        source = lax.rem(row + rows - d, rows)
        value = None
        for g, (lo, hi) in enumerate(bounds):
            if g > 0:
                b_copies[g - 1][d - 1].wait_send()
            if g == len(bounds) - 1:
                reduced.append(over_cols(d - 1))
            b_copies[g][d - 1].wait_recv()
            term = product(lo, hi, source)
            value = term if value is None else value + term
        over_reps(d, value)
    reduced.append(over_cols(rows - 1))

    last = pltpu.make_async_remote_copy(
        src_ref=c_inbox, dst_ref=c_inbox, send_sem=c_send, recv_sem=c_recv,
        device_id={"col": col_at(1)}, device_id_type=MESH)
    last.wait_recv()
    result = mine[...]
    for i in range(cols - 1):
        result = result + c_inbox[i]
    o_ref[...] = result

    for copy in b_copies[-1] + reduced + [last]:
        copy.wait_send()


def local(sizes, amplitudes, integrals):
    rows, cols, reps = sizes
    height, depth, virtuals = amplitudes.shape
    width, lanes = integrals.shape[1:]
    group = cols * reps
    share = rows * lanes // group
    near = cols // rows
    chunks = len(chunk_bounds(depth))
    split = width % 128 != 0
    blocks = jnp.transpose(amplitudes, (1, 0, 2))
    if split:
        blocks = jnp.transpose(blocks.reshape(depth, height, cols, width), (2, 0, 1, 3))
    dma = pltpu.SemaphoreType.DMA
    summed = pl.pallas_call(
        functools.partial(kernel, sizes, split),
        out_shape=jax.ShapeDtypeStruct((share, cols * height), jnp.float32),
        in_specs=[pl.BlockSpec(memory_space=pl.ANY)] * 2,
        out_specs=pl.BlockSpec(memory_space=pltpu.VMEM),
        scratch_shapes=[
            pltpu.VMEM((cols, depth, height, width), amplitudes.dtype),
            pltpu.VMEM((rows, depth, width, lanes), integrals.dtype),
            pltpu.VMEM((rows, reps, near, share, cols * height), jnp.float32),
            pltpu.VMEM((rows, reps - 1, near, share, cols * height), jnp.float32),
            pltpu.VMEM((rows, near, share, cols * height), jnp.float32),
            pltpu.VMEM((cols - 1, share, cols * height), jnp.float32),
            pltpu.VMEM((share, cols * height), jnp.float32),
            dma((max(cols - 1, 1), chunks)),
            dma((max(cols - 1, 1), chunks)),
            dma((max(rows - 1, 1), chunks)),
            dma((max(rows - 1, 1), chunks)),
            dma((rows,)),
            dma((rows,)),
            dma,
            dma,
            dma((2,)),
        ],
        compiler_params=pltpu.CompilerParams(
            collective_id=0, has_side_effects=True, vmem_limit_bytes=56 * 1024 * 1024),
        cost_estimate=pl.CostEstimate(
            flops=2 * cols * height * rows * lanes * depth * width,
            bytes_accessed=2 * (amplitudes.size + integrals.size), transcendentals=0),
    )(blocks, integrals)
    return summed.T


def solution(mesh):
    sizes = (mesh.shape["row"], mesh.shape["col"], mesh.shape["rep"])
    return jax.shard_map(
        functools.partial(local, sizes),
        mesh=mesh,
        in_specs=(P(("row", "col"), "rep", None), P("rep", "col", "row")),
        out_specs=P("row", ("col", "rep")),
        check_vma=False,
    )
```

```python
import functools

import jax
import jax.numpy as jnp
from jax import lax
from jax.experimental import pallas as pl
from jax.experimental.pallas import tpu as pltpu
from jax.sharding import PartitionSpec as P

MESH = pl.DeviceIdType.MESH


def chunk_bounds(depth):
    edges = sorted({0, depth * 6 // 25, depth * 12 // 25, depth * 18 // 25, depth * 22 // 25, depth - 1, depth})
    return list(zip(edges[:-1], edges[1:]))


def packing(share, total_rows):
    full = total_rows // 128 * 128
    packed = 2 * (total_rows - full) == 128 and share % 16 == 0
    return full, packed


def pack(value, per, share, full):
    low = value[:, :full].reshape(per, share, full)
    high = value[:, full:].reshape(per, 2, share // 2, value.shape[1] - full)
    high = jnp.concatenate([high[:, 0], high[:, 1]], axis=2)
    return [low[:, :, i:i + 128] for i in range(0, full, 128)] + [high]


def unpack(value, share, full):
    low = [value[i * share:(i + 1) * share] for i in range(full // 128)]
    high = value[full // 128 * share:]
    high = jnp.concatenate([high[:, :64], high[:, 64:]], axis=0)
    return jnp.concatenate(low + [high], axis=1)


def kernel(sizes, split, a_ref, b_ref, o_ref, a_buf, b_buf, parts, inbox,
           a_send, a_recv, b_send, b_recv, p_send, p_recv, own_sem):
    rows, cols, reps = sizes
    row, col, rep = lax.axis_index("row"), lax.axis_index("col"), lax.axis_index("rep")
    group = cols * reps
    me = col * reps + rep
    depth, height, width = a_buf.shape[1:]
    lanes = b_buf.shape[3]
    per = group // rows
    total_rows = cols * height
    share = o_ref.shape[0]
    full, packed = packing(share, total_rows)
    bounds = chunk_bounds(depth)

    def row_at(d):
        return lax.rem(row + d, rows)

    def col_at(d):
        return lax.rem(col + d, cols)

    barrier = pltpu.get_barrier_semaphore()
    for d in range(1, rows):
        pl.semaphore_signal(barrier, inc=1, device_id={"row": row_at(d)}, device_id_type=MESH)
    for d in range(1, group):
        other = lax.rem(me + d, group)
        pl.semaphore_signal(barrier, inc=1, device_id={"col": other // reps, "rep": lax.rem(other, reps)},
                            device_id_type=MESH)

    def piece(lo, hi, owner):
        if split:
            return a_ref.at[owner, lo:hi]
        return a_ref.at[lo:hi, :, pl.ds(pl.multiple_of(owner * width, width), width)]

    own_a = pltpu.make_async_copy(piece(0, depth, col), a_buf.at[col], own_sem.at[0])
    own_b = pltpu.make_async_copy(b_ref, b_buf.at[row], own_sem.at[1])
    pl.semaphore_wait(barrier, rows - 1 + group - 1)

    a_copies, b_copies = [], []
    for g, (lo, hi) in enumerate(bounds):
        b_copies.append([])
        for d in range(1, rows):
            copy = pltpu.make_async_remote_copy(
                src_ref=b_ref.at[lo:hi], dst_ref=b_buf.at[row, lo:hi],
                send_sem=b_send.at[d - 1, g], recv_sem=b_recv.at[d - 1, g],
                device_id={"row": row_at(d)}, device_id_type=MESH)
            copy.start()
            b_copies[-1].append(copy)
    for g, (lo, hi) in enumerate(bounds):
        a_copies.append([])
        for d in range(1, cols):
            copy = pltpu.make_async_remote_copy(
                src_ref=piece(lo, hi, col_at(d)), dst_ref=a_buf.at[col, lo:hi],
                send_sem=a_send.at[d - 1, g], recv_sem=a_recv.at[d - 1, g],
                device_id={"col": col_at(d)}, device_id_type=MESH)
            copy.start()
            a_copies[-1].append(copy)

    own_a.start()
    own_b.start()

    def product(lo, hi, source):
        left = jnp.concatenate(
            [jnp.concatenate([a_buf[c, k] for c in range(cols)], axis=0) for k in range(lo, hi)], axis=1)
        right = jnp.concatenate([b_buf[source, k] for k in range(lo, hi)], axis=0)
        return jnp.dot(left, right, preferred_element_type=jnp.float32)

    def part_copy(owner):
        return pltpu.make_async_remote_copy(
            src_ref=parts.at[owner], dst_ref=inbox.at[lax.rem(owner - me + group, group) - 1],
            send_sem=p_send, recv_sem=p_recv,
            device_id={"col": owner // reps, "rep": lax.rem(owner, reps)}, device_id_type=MESH)

    def hand_out(source, value):
        if packed:
            start = 0
            for block in pack(value.T, per, share, full):
                parts[pl.ds(source * per, per), start:start + block.shape[1]] = block
                start += block.shape[1]
        else:
            parts[pl.ds(source * per, per)] = value.T.reshape(per, share, total_rows)
        for i in range(per):
            owner = source * per + i // reps * reps + lax.rem(2 * reps - 1 - rep - i % reps, reps)

            @pl.when(owner != me)
            def _():
                part_copy(owner).start()

    own_a.wait()
    own_b.wait()
    value = None
    for g, (lo, hi) in enumerate(bounds):
        for copy in a_copies[g]:
            copy.wait_recv()
        term = product(lo, hi, row)
        value = term if value is None else value + term
    hand_out(row, value)

    for copies in a_copies:
        for copy in copies:
            copy.wait_send()

    for d in range(1, rows):
        source = lax.rem(row + rows - d, rows)
        value = None
        for g, (lo, hi) in enumerate(bounds):
            if g > 0:
                b_copies[g - 1][d - 1].wait_send()
            b_copies[g][d - 1].wait_recv()
            term = product(lo, hi, source)
            value = term if value is None else value + term
        hand_out(source, value)

    pieces = pltpu.make_async_remote_copy(
        src_ref=parts.at[0:group - 1], dst_ref=inbox, send_sem=p_send, recv_sem=p_recv,
        device_id={"col": col_at(1)}, device_id_type=MESH)
    pieces.wait_recv()
    result = parts[me]
    for i in range(group - 1):
        result = result + inbox[i]
    o_ref[...] = unpack(result, share, full) if packed else result

    for copy in b_copies[-1]:
        copy.wait_send()
    pieces.wait_send()


def local(sizes, amplitudes, integrals):
    rows, cols, reps = sizes
    height, depth, virtuals = amplitudes.shape
    width, lanes = integrals.shape[1:]
    group = cols * reps
    share = rows * lanes // group
    tile = (share, cols * height)
    if packing(*tile)[1]:
        tile = (share * cols * height // 128, 128)
    chunks = len(chunk_bounds(depth))
    split = width % 128 != 0
    blocks = jnp.transpose(amplitudes, (1, 0, 2))
    if split:
        blocks = jnp.transpose(blocks.reshape(depth, height, cols, width), (2, 0, 1, 3))
    dma = pltpu.SemaphoreType.DMA
    summed = pl.pallas_call(
        functools.partial(kernel, sizes, split),
        out_shape=jax.ShapeDtypeStruct((share, cols * height), jnp.float32),
        in_specs=[pl.BlockSpec(memory_space=pl.ANY)] * 2,
        out_specs=pl.BlockSpec(memory_space=pltpu.VMEM),
        scratch_shapes=[
            pltpu.VMEM((cols, depth, height, width), amplitudes.dtype),
            pltpu.VMEM((rows, depth, width, lanes), integrals.dtype),
            pltpu.VMEM((group,) + tile, jnp.float32),
            pltpu.VMEM((group - 1,) + tile, jnp.float32),
            dma((max(cols - 1, 1), chunks)),
            dma((max(cols - 1, 1), chunks)),
            dma((max(rows - 1, 1), chunks)),
            dma((max(rows - 1, 1), chunks)),
            dma,
            dma,
            dma((2,)),
        ],
        compiler_params=pltpu.CompilerParams(
            collective_id=0, has_side_effects=True, vmem_limit_bytes=56 * 1024 * 1024),
        cost_estimate=pl.CostEstimate(
            flops=2 * cols * height * rows * lanes * depth * width,
            bytes_accessed=2 * (amplitudes.size + integrals.size), transcendentals=0),
    )(blocks, integrals)
    return summed.T


def solution(mesh):
    sizes = (mesh.shape["row"], mesh.shape["col"], mesh.shape["rep"])
    return jax.shard_map(
        functools.partial(local, sizes),
        mesh=mesh,
        in_specs=(P(("row", "col"), "rep", None), P("rep", "col", "row")),
        out_specs=P("row", ("col", "rep")),
        check_vma=False,
    )
```

```python
import functools

import jax
import jax.numpy as jnp
from jax import lax
from jax.experimental import pallas as pl
from jax.experimental.pallas import tpu as pltpu
from jax.sharding import PartitionSpec as P

MESH = pl.DeviceIdType.MESH


def chunk_bounds(depth):
    edges = sorted({0, depth * 6 // 25, depth * 12 // 25, depth * 18 // 25, depth * 22 // 25, depth - 1, depth})
    return list(zip(edges[:-1], edges[1:]))


def packing(share, total_rows):
    full = total_rows // 128 * 128
    packed = 2 * (total_rows - full) == 128 and share % 16 == 0
    return full, packed


def pack(value, per, share, full):
    low = value[:, :full].reshape(per, share, full)
    high = value[:, full:].reshape(per, 2, share // 2, value.shape[1] - full)
    high = jnp.concatenate([high[:, 0], high[:, 1]], axis=2)
    return [low[:, :, i:i + 128] for i in range(0, full, 128)] + [high]


def unpack(value, share, full):
    low = [value[i * share:(i + 1) * share] for i in range(full // 128)]
    high = value[full // 128 * share:]
    high = jnp.concatenate([high[:, :64], high[:, 64:]], axis=0)
    return jnp.concatenate(low + [high], axis=1)


def kernel(sizes, split, a_ref, b_ref, o_ref, a_buf, b_buf, parts, inbox,
           a_send, a_recv, b_send, b_recv, p_send, p_recv, own_sem):
    rows, cols, reps = sizes
    row, col, rep = lax.axis_index("row"), lax.axis_index("col"), lax.axis_index("rep")
    group = cols * reps
    me = col * reps + rep
    depth, height, width = a_buf.shape[1:]
    lanes = b_buf.shape[3]
    per = group // rows
    total_rows = cols * height
    share = o_ref.shape[0]
    full, packed = packing(share, total_rows)
    bounds = chunk_bounds(depth)

    def row_at(d):
        return lax.rem(row + d, rows)

    def col_at(d):
        return lax.rem(col + d, cols)

    barrier = pltpu.get_barrier_semaphore()
    for d in range(1, rows):
        pl.semaphore_signal(barrier, inc=1, device_id={"row": row_at(d)}, device_id_type=MESH)
    for d in range(1, group):
        other = lax.rem(me + d, group)
        pl.semaphore_signal(barrier, inc=1, device_id={"col": other // reps, "rep": lax.rem(other, reps)},
                            device_id_type=MESH)

    def piece(lo, hi, owner):
        if split:
            return a_ref.at[owner, lo:hi]
        return a_ref.at[lo:hi, :, pl.ds(pl.multiple_of(owner * width, width), width)]

    own_a = pltpu.make_async_copy(piece(0, depth, col), a_buf.at[col], own_sem.at[0])
    own_b = pltpu.make_async_copy(b_ref, b_buf.at[row], own_sem.at[1])
    pl.semaphore_wait(barrier, rows - 1 + group - 1)

    a_copies, b_copies = [], []
    for g, (lo, hi) in enumerate(bounds):
        b_copies.append([])
        for d in range(1, rows):
            copy = pltpu.make_async_remote_copy(
                src_ref=b_ref.at[lo:hi], dst_ref=b_buf.at[row, lo:hi],
                send_sem=b_send.at[d - 1, g], recv_sem=b_recv.at[d - 1, g],
                device_id={"row": row_at(d)}, device_id_type=MESH)
            copy.start()
            b_copies[-1].append(copy)
    for g, (lo, hi) in enumerate(bounds):
        a_copies.append([])
        for d in range(1, cols):
            copy = pltpu.make_async_remote_copy(
                src_ref=piece(lo, hi, col_at(d)), dst_ref=a_buf.at[col, lo:hi],
                send_sem=a_send.at[d - 1, g], recv_sem=a_recv.at[d - 1, g],
                device_id={"col": col_at(d)}, device_id_type=MESH)
            copy.start()
            a_copies[-1].append(copy)

    own_a.start()
    own_b.start()

    def product(lo, hi, source):
        left = jnp.concatenate(
            [jnp.concatenate([a_buf[c, k] for c in range(cols)], axis=0) for k in range(lo, hi)], axis=1)
        right = jnp.concatenate([b_buf[source, k] for k in range(lo, hi)], axis=0)
        return jnp.dot(left, right, preferred_element_type=jnp.float32)

    def part_copy(owner):
        return pltpu.make_async_remote_copy(
            src_ref=parts.at[owner], dst_ref=inbox.at[lax.rem(owner - me + group, group) - 1],
            send_sem=p_send, recv_sem=p_recv,
            device_id={"col": owner // reps, "rep": lax.rem(owner, reps)}, device_id_type=MESH)

    def hand_out(source, value):
        if packed:
            start = 0
            for block in pack(value.T, per, share, full):
                parts[pl.ds(source * per, per), start:start + block.shape[1]] = block
                start += block.shape[1]
        else:
            parts[pl.ds(source * per, per)] = value.T.reshape(per, share, total_rows)
        for i in range(per):
            owner = source * per + i // reps * reps + lax.rem(2 * reps - 1 - rep - i % reps, reps)

            @pl.when(owner != me)
            def _():
                part_copy(owner).start()

    own_a.wait()
    own_b.wait()
    value = None
    for g, (lo, hi) in enumerate(bounds):
        for copy in a_copies[g]:
            copy.wait_recv()
        term = product(lo, hi, row)
        value = term if value is None else value + term
    hand_out(row, value)

    for copies in a_copies:
        for copy in copies:
            copy.wait_send()

    for d in range(1, rows):
        source = lax.rem(row + rows - d, rows)
        value = None
        for g, (lo, hi) in enumerate(bounds):
            if g > 0:
                b_copies[g - 1][d - 1].wait_send()
            b_copies[g][d - 1].wait_recv()
            term = product(lo, hi, source)
            value = term if value is None else value + term
        hand_out(source, value)

    pieces = pltpu.make_async_remote_copy(
        src_ref=parts.at[0:group - 1], dst_ref=inbox, send_sem=p_send, recv_sem=p_recv,
        device_id={"col": col_at(1)}, device_id_type=MESH)
    pieces.wait_recv()
    result = parts[me]
    for i in range(group - 1):
        result = result + inbox[i]
    o_ref[...] = unpack(result, share, full) if packed else result

    for copy in b_copies[-1]:
        copy.wait_send()
    pieces.wait_send()


def local(sizes, amplitudes, integrals):
    rows, cols, reps = sizes
    height, depth, virtuals = amplitudes.shape
    width, lanes = integrals.shape[1:]
    group = cols * reps
    share = rows * lanes // group
    tile = (share, cols * height)
    if packing(*tile)[1]:
        tile = (share * cols * height // 128, 128)
    chunks = len(chunk_bounds(depth))
    split = width % 128 != 0
    blocks = jnp.transpose(amplitudes, (1, 0, 2))
    if split:
        blocks = jnp.transpose(blocks.reshape(depth, height, cols, width), (2, 0, 1, 3))
    dma = pltpu.SemaphoreType.DMA
    summed = pl.pallas_call(
        functools.partial(kernel, sizes, split),
        out_shape=jax.ShapeDtypeStruct((share, cols * height), jnp.float32),
        in_specs=[pl.BlockSpec(memory_space=pl.ANY)] * 2,
        out_specs=pl.BlockSpec(memory_space=pltpu.VMEM),
        scratch_shapes=[
            pltpu.VMEM((cols, depth, height, width), amplitudes.dtype),
            pltpu.VMEM((rows, depth, width, lanes), integrals.dtype),
            pltpu.VMEM((group,) + tile, jnp.float32),
            pltpu.VMEM((group - 1,) + tile, jnp.float32),
            dma((max(cols - 1, 1), chunks)),
            dma((max(cols - 1, 1), chunks)),
            dma((max(rows - 1, 1), chunks)),
            dma((max(rows - 1, 1), chunks)),
            dma,
            dma,
            dma((2,)),
        ],
        compiler_params=pltpu.CompilerParams(
            collective_id=0, has_side_effects=True, vmem_limit_bytes=53 * 1024 * 1024),
        cost_estimate=pl.CostEstimate(
            flops=2 * cols * height * rows * lanes * depth * width,
            bytes_accessed=2 * (amplitudes.size + integrals.size), transcendentals=0),
    )(blocks, integrals)
    return summed.T


def solution(mesh):
    sizes = (mesh.shape["row"], mesh.shape["col"], mesh.shape["rep"])
    return jax.shard_map(
        functools.partial(local, sizes),
        mesh=mesh,
        in_specs=(P(("row", "col"), "rep", None), P("rep", "col", "row")),
        out_specs=P("row", ("col", "rep")),
        check_vma=False,
    )
```

```python
import functools

import jax
import jax.numpy as jnp
from jax import lax
from jax.experimental import pallas as pl
from jax.experimental.pallas import tpu as pltpu
from jax.sharding import PartitionSpec as P

MESH = pl.DeviceIdType.MESH


def chunk_bounds(depth):
    edges = sorted({0, depth * 6 // 25, depth * 12 // 25, depth * 18 // 25, depth * 22 // 25, depth - 1, depth})
    return list(zip(edges[:-1], edges[1:]))


def packing(share, total_rows):
    full = total_rows // 128 * 128
    packed = 2 * (total_rows - full) == 128 and share % 16 == 0
    return full, packed


def pack(value, per, share, full):
    low = value[:, :full].reshape(per, share, full)
    high = value[:, full:].reshape(per, 2, share // 2, value.shape[1] - full)
    high = jnp.concatenate([high[:, 0], high[:, 1]], axis=2)
    return [low[:, :, i:i + 128] for i in range(0, full, 128)] + [high]


def unpack(value, share, full):
    low = [value[i * share:(i + 1) * share] for i in range(full // 128)]
    high = value[full // 128 * share:]
    high = jnp.concatenate([high[:, :64], high[:, 64:]], axis=0)
    return jnp.concatenate(low + [high], axis=1)


def kernel(sizes, split, a_ref, b_ref, o_ref, a_buf, b_buf, parts, inbox,
           a_send, a_recv, b_send, b_recv, p_send, p_recv, own_sem):
    rows, cols, reps = sizes
    row, col, rep = lax.axis_index("row"), lax.axis_index("col"), lax.axis_index("rep")
    group = cols * reps
    me = col * reps + rep
    depth, height, width = a_buf.shape[1:]
    lanes = b_buf.shape[3]
    per = group // rows
    total_rows = cols * height
    share = o_ref.shape[0]
    full, packed = packing(share, total_rows)
    bounds = chunk_bounds(depth)

    def row_at(d):
        return lax.rem(row + d, rows)

    def col_at(d):
        return lax.rem(col + d, cols)

    barrier = pltpu.get_barrier_semaphore()
    for d in range(1, rows):
        pl.semaphore_signal(barrier, inc=1, device_id={"row": row_at(d)}, device_id_type=MESH)
    for d in range(1, group):
        other = lax.rem(me + d, group)
        pl.semaphore_signal(barrier, inc=1, device_id={"col": other // reps, "rep": lax.rem(other, reps)},
                            device_id_type=MESH)

    def piece(lo, hi, owner):
        if split:
            return a_ref.at[owner, lo:hi]
        return a_ref.at[lo:hi, :, pl.ds(pl.multiple_of(owner * width, width), width)]

    own_a = pltpu.make_async_copy(piece(0, depth, col), a_buf.at[col], own_sem.at[0])
    own_b = pltpu.make_async_copy(b_ref, b_buf.at[row], own_sem.at[1])
    pl.semaphore_wait(barrier, rows - 1 + group - 1)

    a_copies, b_copies = [], []
    for g, (lo, hi) in enumerate(bounds):
        b_copies.append([])
        for d in range(1, rows):
            copy = pltpu.make_async_remote_copy(
                src_ref=b_ref.at[lo:hi], dst_ref=b_buf.at[row, lo:hi],
                send_sem=b_send.at[d - 1, g], recv_sem=b_recv.at[d - 1, g],
                device_id={"row": row_at(d)}, device_id_type=MESH)
            copy.start()
            b_copies[-1].append(copy)
    for g, (lo, hi) in enumerate(bounds):
        a_copies.append([])
        for d in range(1, cols):
            copy = pltpu.make_async_remote_copy(
                src_ref=piece(lo, hi, col_at(d)), dst_ref=a_buf.at[col, lo:hi],
                send_sem=a_send.at[d - 1, g], recv_sem=a_recv.at[d - 1, g],
                device_id={"col": col_at(d)}, device_id_type=MESH)
            copy.start()
            a_copies[-1].append(copy)

    own_a.start()
    own_b.start()

    def product(lo, hi, source):
        left = jnp.concatenate(
            [jnp.concatenate([a_buf[c, k] for c in range(cols)], axis=0) for k in range(lo, hi)], axis=1)
        right = jnp.concatenate([b_buf[source, k] for k in range(lo, hi)], axis=0)
        return jnp.dot(left, right, preferred_element_type=jnp.float32)

    def part_copy(owner):
        return pltpu.make_async_remote_copy(
            src_ref=parts.at[owner], dst_ref=inbox.at[lax.rem(owner - me + group, group) - 1],
            send_sem=p_send, recv_sem=p_recv,
            device_id={"col": owner // reps, "rep": lax.rem(owner, reps)}, device_id_type=MESH)

    def hand_out(source, value):
        for first in range(0, per, reps):
            block = value[:, first * share:(first + reps) * share].T
            place = pl.ds(source * per + first, reps)
            if packed:
                start = 0
                for part in pack(block, reps, share, full):
                    parts[place, start:start + part.shape[1]] = part
                    start += part.shape[1]
            else:
                parts[place] = block.reshape(reps, share, total_rows)
            for i in range(reps):
                owner = source * per + first + lax.rem(2 * reps - 1 - rep - i, reps)

                @pl.when(owner != me)
                def _():
                    part_copy(owner).start()

    own_a.wait()
    own_b.wait()
    value = None
    for g, (lo, hi) in enumerate(bounds):
        for copy in a_copies[g]:
            copy.wait_recv()
        term = product(lo, hi, row)
        value = term if value is None else value + term
    hand_out(row, value)

    for copies in a_copies:
        for copy in copies:
            copy.wait_send()

    for d in range(1, rows):
        source = lax.rem(row + rows - d, rows)
        value = None
        for g, (lo, hi) in enumerate(bounds):
            if g > 0:
                b_copies[g - 1][d - 1].wait_send()
            b_copies[g][d - 1].wait_recv()
            term = product(lo, hi, source)
            value = term if value is None else value + term
        hand_out(source, value)

    pieces = pltpu.make_async_remote_copy(
        src_ref=parts.at[0:group - 1], dst_ref=inbox, send_sem=p_send, recv_sem=p_recv,
        device_id={"col": col_at(1)}, device_id_type=MESH)
    pieces.wait_recv()
    result = parts[me]
    for i in range(group - 1):
        result = result + inbox[i]
    o_ref[...] = unpack(result, share, full) if packed else result

    for copy in b_copies[-1]:
        copy.wait_send()
    pieces.wait_send()


def local(sizes, amplitudes, integrals):
    rows, cols, reps = sizes
    height, depth, virtuals = amplitudes.shape
    width, lanes = integrals.shape[1:]
    group = cols * reps
    share = rows * lanes // group
    tile = (share, cols * height)
    if packing(*tile)[1]:
        tile = (share * cols * height // 128, 128)
    chunks = len(chunk_bounds(depth))
    split = width % 128 != 0
    blocks = jnp.transpose(amplitudes, (1, 0, 2))
    if split:
        blocks = jnp.transpose(blocks.reshape(depth, height, cols, width), (2, 0, 1, 3))
    dma = pltpu.SemaphoreType.DMA
    summed = pl.pallas_call(
        functools.partial(kernel, sizes, split),
        out_shape=jax.ShapeDtypeStruct((share, cols * height), jnp.float32),
        in_specs=[pl.BlockSpec(memory_space=pl.ANY)] * 2,
        out_specs=pl.BlockSpec(memory_space=pltpu.VMEM),
        scratch_shapes=[
            pltpu.VMEM((cols, depth, height, width), amplitudes.dtype),
            pltpu.VMEM((rows, depth, width, lanes), integrals.dtype),
            pltpu.VMEM((group,) + tile, jnp.float32),
            pltpu.VMEM((group - 1,) + tile, jnp.float32),
            dma((max(cols - 1, 1), chunks)),
            dma((max(cols - 1, 1), chunks)),
            dma((max(rows - 1, 1), chunks)),
            dma((max(rows - 1, 1), chunks)),
            dma,
            dma,
            dma((2,)),
        ],
        compiler_params=pltpu.CompilerParams(
            collective_id=0, has_side_effects=True, vmem_limit_bytes=53 * 1024 * 1024),
        cost_estimate=pl.CostEstimate(
            flops=2 * cols * height * rows * lanes * depth * width,
            bytes_accessed=2 * (amplitudes.size + integrals.size), transcendentals=0),
    )(blocks, integrals)
    return summed.T


def solution(mesh):
    sizes = (mesh.shape["row"], mesh.shape["col"], mesh.shape["rep"])
    return jax.shard_map(
        functools.partial(local, sizes),
        mesh=mesh,
        in_specs=(P(("row", "col"), "rep", None), P("rep", "col", "row")),
        out_specs=P("row", ("col", "rep")),
        check_vma=False,
    )
```
